256 devices in a mesh: patch: 32 (over z, y_hi, core), uly: 8 (over y_lo, x).
Axes of the slice: x: 4, y: 4 (y_hi: 2, y_lo: 2; y = y_hi * 2 + y_lo), z: 8, core: 2. Of those that a mesh axis runs over, the one named last changes fastest.
Arguments:
- query: bfloat16 [12288, 3072], P(('patch', 'uly')), may hold values from -8 to 8
- key_fresh: bfloat16 [12288, 3072], P(('patch', 'uly')), may hold values from -8 to 8
- value_fresh: bfloat16 [12288, 3072], P(('patch', 'uly')), may hold values from -6 to 6
- key_stale: bfloat16 [12288, 3072], P(('patch', 'uly')), may hold values from -8 to 8
- value_stale: bfloat16 [12288, 3072], P(('patch', 'uly')), may hold values from -6 to 6
Outputs:
- attended: bfloat16 [12288, 3072], P(('patch', 'uly'))
The draws below stay inside these ranges and needn't reach their ends.
All inputs are finite; a program needn't handle non-finite values.
Results may differ from the reference program's by a relative error of at most 0.006.
Values may be sent and summed in bfloat16 or wider, within the bound.
A program may use at most 64 MiB of HBM per device.

```python
import jax
import jax.numpy as jnp
from jax import lax

HD = 128
HEADS = 24
SPAN = 384
TOKENS = 12288
N_PATCH = 32


def draw_query(key, part):
    key = jax.random.fold_in(key, 11)
    result = jnp.clip(2.5 * jax.random.normal(key, (TOKENS, HEADS * HD), jnp.float32), -8.0, 8.0)
    return result.astype(jnp.bfloat16)


def draw_key_stale(key, part):
    key = jax.random.fold_in(key, 23)
    result = jnp.clip(jax.random.normal(key, (TOKENS, HEADS * HD), jnp.float32), -8.0, 8.0)
    return result.astype(jnp.bfloat16)


def levels(key, shape, pieces, least, high):
    loudness = 1.0
    for dim, blocks in pieces:
        heights = jax.random.uniform(jax.random.fold_in(jax.random.fold_in(key, 6), dim), (blocks,), jnp.float32, least / len(pieces), high / len(pieces))
        loudness = loudness * jnp.repeat(jnp.exp(heights), shape[dim] // blocks).reshape((-1,) + (1,) * (len(shape) - 1 - dim))
    return loudness


def normal_values(own_key, extent, deviation, most, pieces=(), kind=jnp.bfloat16):
    loudness = levels(own_key, extent, pieces, -0.22, 0.18) if pieces else 1.0
    values = jax.random.normal(own_key, extent, jnp.float32) * deviation * loudness
    return jnp.minimum(jnp.maximum(values, -most), most).astype(kind)


def setup_inputs(seed: int = 0) -> dict:
    streams_of = jax.random.split(jax.random.key(seed), 6)
    query = draw_query(jax.random.fold_in(streams_of[5], 71), 0)
    key_fresh = normal_values(streams_of[1], (TOKENS, HEADS * HD), 1.0, 8.0, ((0, 256),))
    value_fresh = normal_values(streams_of[2], (TOKENS, HEADS * HD), 1.0, 6.0, ((0, 256),))
    key_stale = draw_key_stale(jax.random.fold_in(streams_of[5], 71), 0)
    value_stale = normal_values(streams_of[4], (TOKENS, HEADS * HD), 1.0, 6.0, ((0, 256),))
    return {"query": query, "key_fresh": key_fresh, "value_fresh": value_fresh, "key_stale": key_stale, "value_stale": value_stale}


def reference(query, key_fresh, value_fresh, key_stale, value_stale):
    score_scale = HD ** -0.5
    shaped_query = query.reshape(TOKENS, HEADS, HD)
    shaped_kfresh = key_fresh.reshape(TOKENS, HEADS, HD)
    shaped_vfresh = value_fresh.reshape(TOKENS, HEADS, HD)
    shaped_kstale = key_stale.reshape(TOKENS, HEADS, HD).astype(jnp.float32)
    shaped_vstale = value_stale.reshape(TOKENS, HEADS, HD).astype(jnp.float32)

    def one_patch(patch_index):
        first_row = (patch_index * SPAN).astype(jnp.int32)
        queries = lax.dynamic_slice_in_dim(shaped_query, first_row, SPAN, 0).astype(jnp.float32)
        own_keys = lax.dynamic_slice_in_dim(shaped_kfresh, first_row, SPAN, 0).astype(jnp.float32)
        own_values = lax.dynamic_slice_in_dim(shaped_vfresh, first_row, SPAN, 0).astype(jnp.float32)
        all_keys = lax.dynamic_update_slice_in_dim(shaped_kstale, own_keys, first_row, 0)
        all_values = lax.dynamic_update_slice_in_dim(shaped_vstale, own_values, first_row, 0)
        scores = jnp.einsum("qhd,khd->hqk", queries, all_keys) * score_scale
        top_score = jnp.max(scores, axis=-1)
        weights = jnp.exp(scores - top_score[:, :, None])
        total = jnp.sum(weights, axis=-1)
        rounded = weights.astype(jnp.bfloat16).astype(jnp.float32)
        summed = jnp.einsum("hqk,khd->qhd", rounded, all_values)
        return (summed / jnp.transpose(total)[:, :, None]).astype(jnp.bfloat16)

    stacked = lax.map(one_patch, jnp.arange(N_PATCH, dtype=jnp.int32))
    return stacked.reshape(TOKENS, HEADS * HD)
```

```python
import functools
import math

import jax
import jax.numpy as jnp
from jax import lax
from jax.experimental import pallas as pl
from jax.experimental.pallas import tpu as pltpu
from jax.sharding import PartitionSpec as P

HD = 128
HPG = 3
WIDTH = HPG * HD
NU = 8
NZ = 8
HALF = NZ // 2
SLICE = 48
SPAN = NU * SLICE
MESH = pl.DeviceIdType.MESH
C2 = HD ** (-0.5) * math.log2(math.e)


def slot_of(d, s):
    if s == 0:
        return 0
    if s == HALF:
        return HALF
    return s if d == 0 else HALF + s


def reach(t, d):
    return HALF if t == d else HALF - 1


def kernel(q_in, kf_in, vf_in, ks_in, vs_in, out_ref,
           qbuf, kfb, vfb, kbuf, vbuf, acc, mx, ls, obuf, sbuf, ob_in, sb_in, res,
           a2a_send, a2a_recv, loc_sem, ring_send, ring_recv, sib_send, sib_recv,
           qp_sem, part_send, part_recv, out_send, out_recv, out_loc):
    patch = lax.axis_index("patch")
    u = lax.axis_index("uly")
    z = patch // 4
    yh = (patch // 2) % 2
    c = patch % 2
    up = ((z + 1) % NZ) * 4 + yh * 2 + c
    down = ((z + NZ - 1) % NZ) * 4 + yh * 2 + c
    sib = z * 4 + yh * 2 + (1 - c)
    par = z * 4 + (1 - yh) * 2 + c
    crow = pl.ds(pl.multiple_of(c * SPAN, SPAN), SPAN)
    orow = pl.ds(pl.multiple_of((1 - c) * SPAN, SPAN), SPAN)

    barrier = pltpu.get_barrier_semaphore()
    for o in range(1, NU):
        pl.semaphore_signal(barrier, inc=1, device_id=(patch, (u + o) % NU), device_id_type=MESH)
    for p in (up, down, sib, par):
        pl.semaphore_signal(barrier, inc=1, device_id=(p, u), device_id_type=MESH)
    pl.semaphore_wait(barrier, NU - 1 + 4)

    def cols(h):
        return pl.ds(pl.multiple_of(h * HD, HD), HD)

    ins = (ks_in, vs_in, q_in, kf_in, vf_in)
    own_rows = pl.ds(pl.multiple_of(u * SLICE, SLICE), SLICE)

    def landing(i):
        if i == 0:
            return kbuf.at[0, crow]
        if i == 1:
            return vbuf.at[0, crow]
        return (qbuf.at[pl.ds(0, SPAN)], kfb, vfb)[i - 2]

    def place(i):
        rows = pl.ds(pl.multiple_of(c * SPAN + u * SLICE, SLICE), SLICE)
        if i == 0:
            return kbuf.at[0, rows]
        if i == 1:
            return vbuf.at[0, rows]
        return (qbuf, kfb, vfb)[i - 2].at[own_rows]

    def a2a(i, o):
        peer = (u + o) % NU
        src = ins[i].at[:, pl.ds(pl.multiple_of(peer * WIDTH, WIDTH), WIDTH)]
        return pltpu.make_async_remote_copy(
            src_ref=src, dst_ref=place(i), send_sem=a2a_send.at[i, o], recv_sem=a2a_recv.at[i, o],
            device_id=(patch, peer), device_id_type=MESH)

    def local(i):
        src = ins[i].at[:, pl.ds(pl.multiple_of(u * WIDTH, WIDTH), WIDTH)]
        return pltpu.make_async_copy(src, place(i), loc_sem.at[i])

    for i in range(5):
        for o in range(1, NU):
            a2a(i, o).start()
        local(i).start()

    def a2a_wait(i):
        for o in range(1, NU):
            a2a(i, o).wait_recv()
        local(i).wait()

    bufs = (kbuf, vbuf)

    def ring(t, d, s, h):
        return pltpu.make_async_remote_copy(
            src_ref=bufs[t].at[slot_of(d, s - 1), crow, cols(h)],
            dst_ref=bufs[t].at[slot_of(d, s), crow, cols(h)],
            send_sem=ring_send.at[t, d, s - 1, h], recv_sem=ring_recv.at[t, d, s - 1, h],
            device_id=(up if d == 0 else down, u), device_id_type=MESH)

    def to_sib(t, slot, h):
        return pltpu.make_async_remote_copy(
            src_ref=bufs[t].at[slot, crow, cols(h)], dst_ref=bufs[t].at[slot, crow, cols(h)],
            send_sem=sib_send.at[t, slot, h], recv_sem=sib_recv.at[t, slot, h],
            device_id=(sib, u), device_id_type=MESH)

    def heads(body):
        def step(h, carry):
            body(h)
            return carry
        lax.fori_loop(0, HPG, step, 0)

    a2a_wait(0)
    a2a_wait(1)

    def launch(h):
        for t in range(2):
            for d in range(2):
                ring(t, d, 1, h).start()
        for t in range(2):
            to_sib(t, 0, h).start()
    heads(launch)

    a2a_wait(2)
    q_par = pltpu.make_async_remote_copy(
        src_ref=qbuf.at[pl.ds(0, SPAN)], dst_ref=qbuf.at[pl.ds(SPAN, SPAN)],
        send_sem=qp_sem.at[0], recv_sem=qp_sem.at[1], device_id=(par, u), device_id_type=MESH)
    q_par.start()

    def attend(h, row0, rows, k, v, first=False):
        n = k.shape[0]
        r = pl.ds(row0, rows)
        s = lax.dot_general(qbuf[r, cols(h)], k, (((1,), (1,)), ((), ())),
                            preferred_element_type=jnp.float32) * C2
        top = jnp.max(s, axis=1, keepdims=True)
        if first:
            m_new = jnp.broadcast_to(top, (rows, HD))
        else:
            m_old = mx[h, r, :]
            m_new = jnp.maximum(m_old, top)
        parts = [jnp.exp2(s[:, j * HD:(j + 1) * HD] - m_new) for j in range(n // HD)]
        tot = parts[0]
        for part in parts[1:]:
            tot = tot + part
        w = jnp.concatenate([part.astype(jnp.bfloat16) for part in parts], axis=1)
        pv = jnp.dot(w, v, preferred_element_type=jnp.float32)
        mx[h, r, :] = m_new
        if first:
            ls[h, r, :] = tot
            acc[h, r, :] = pv
        else:
            alpha = jnp.exp2(m_old - m_new)
            ls[h, r, :] = ls[h, r, :] * alpha + tot
            acc[h, r, :] = acc[h, r, :] * alpha + pv

    TQ = 128

    def attend_rows(h, first_row, count, k, v, first=False):
        for i in range(count // TQ):
            attend(h, first_row + i * TQ, TQ, k, v, first)

    a2a_wait(3)
    a2a_wait(4)
    heads(lambda h: attend_rows(h, 0, SPAN, kfb[:, cols(h)], vfb[:, cols(h)], True))
    q_par.wait_recv()

    def step0(h):
        to_sib(0, 0, h).wait_recv()
        to_sib(1, 0, h).wait_recv()
        attend_rows(h, 0, SPAN, kbuf[0, orow, cols(h)], vbuf[0, orow, cols(h)])
        attend_rows(h, SPAN, SPAN, kbuf[0, :, cols(h)], vbuf[0, :, cols(h)], True)
    heads(step0)

    def arrive(t, d, s, h):
        ring(t, d, s, h).wait_recv()
        if s < reach(t, d):
            ring(t, d, s + 1, h).start()
        to_sib(t, slot_of(d, s), h).start()

    def block(slot, h):
        to_sib(0, slot, h).wait_recv()
        to_sib(1, slot, h).wait_recv()
        attend_rows(h, 0, 2 * SPAN, kbuf[slot, :, cols(h)], vbuf[slot, :, cols(h)])

    for s in range(1, HALF):
        def step(h, s=s):
            for t in range(2):
                for d in range(2):
                    arrive(t, d, s, h)
            for d in range(2):
                block(slot_of(d, s), h)
        heads(step)

    def part_o(h):
        return pltpu.make_async_remote_copy(
            src_ref=obuf.at[h], dst_ref=ob_in.at[h], send_sem=part_send.at[0, h], recv_sem=part_recv.at[0, h],
            device_id=(par, u), device_id_type=MESH)

    def part_s(h):
        return pltpu.make_async_remote_copy(
            src_ref=sbuf.at[h], dst_ref=sb_in.at[h], send_sem=part_send.at[1, h], recv_sem=part_recv.at[1, h],
            device_id=(par, u), device_id_type=MESH)

    def last(h):
        arrive(0, 0, HALF, h)
        arrive(1, 1, HALF, h)
        block(HALF, h)
        r = pl.ds(SPAN, SPAN)
        total = jnp.sum(ls[h, r, :], axis=1, keepdims=True)
        obuf[h] = (acc[h, r, :] / total).astype(jnp.bfloat16)
        lse = mx[h, r, :] + jnp.log2(total)
        for i in range(SPAN // HD):
            sbuf[h, i:i + 1, :] = jnp.transpose(lse[i * HD:(i + 1) * HD, :])[0:1, :]
        for i in range(SPAN // HD, 8):
            sbuf[h, i:i + 1, :] = jnp.zeros((1, HD), jnp.float32)
        part_o(h).start()
        part_s(h).start()
    heads(last)

    def out_copy(h, o):
        peer = (u + o) % NU
        return pltpu.make_async_remote_copy(
            src_ref=res.at[pl.ds(pl.multiple_of(peer * SLICE, SLICE), SLICE), cols(h)],
            dst_ref=out_ref.at[:, pl.ds(pl.multiple_of(u * WIDTH + h * HD, HD), HD)],
            send_sem=out_send.at[h, o], recv_sem=out_recv.at[h, o],
            device_id=(patch, peer), device_id_type=MESH)

    def out_local(h):
        return pltpu.make_async_copy(
            res.at[own_rows, cols(h)],
            out_ref.at[:, pl.ds(pl.multiple_of(u * WIDTH + h * HD, HD), HD)], out_loc.at[h])

    def merge(h):
        part_o(h).wait_recv()
        part_s(h).wait_recv()
        for i in range(SPAN // HD):
            r = pl.ds(i * HD, HD)
            tot_a = jnp.sum(ls[h, r, :], axis=1, keepdims=True)
            lse_a = mx[h, r, :] + jnp.log2(tot_a)
            lse_b = jnp.transpose(jnp.broadcast_to(sb_in[h, i:i + 1, :], (HD, HD)))
            peak = jnp.maximum(lse_a, lse_b)
            wa = jnp.exp2(lse_a - peak)
            wb = jnp.exp2(lse_b - peak)
            both = (wa / tot_a) * acc[h, r, :] + wb * ob_in[h, r, :].astype(jnp.float32)
            res[r, cols(h)] = (both / (wa + wb)).astype(jnp.bfloat16)
        for o in range(1, NU):
            out_copy(h, o).start()
        out_local(h).start()
    heads(merge)

    def finish(h):
        for o in range(1, NU):
            out_copy(h, o).wait()
        out_local(h).wait()
        part_o(h).wait_send()
        part_s(h).wait_send()
        for t in range(2):
            for d in range(2):
                for s in range(1, reach(t, d) + 1):
                    ring(t, d, s, h).wait_send()
            for slot in range(NZ):
                to_sib(t, slot, h).wait_send()
    heads(finish)
    q_par.wait_send()
    for i in range(5):
        for o in range(1, NU):
            a2a(i, o).wait_send()


def shards(query, key_fresh, value_fresh, key_stale, value_stale):
    bf, f32 = jnp.bfloat16, jnp.float32
    dma = pltpu.SemaphoreType.DMA
    return pl.pallas_call(
        kernel,
        out_shape=jax.ShapeDtypeStruct(query.shape, bf),
        in_specs=[pl.BlockSpec(memory_space=pl.ANY)] * 5,
        out_specs=pl.BlockSpec(memory_space=pl.ANY),
        scratch_shapes=[
            pltpu.VMEM((2 * SPAN, WIDTH), bf),
            pltpu.VMEM((SPAN, WIDTH), bf),
            pltpu.VMEM((SPAN, WIDTH), bf),
            pltpu.VMEM((NZ, 2 * SPAN, WIDTH), bf),
            pltpu.VMEM((NZ, 2 * SPAN, WIDTH), bf),
            pltpu.VMEM((HPG, 2 * SPAN, HD), f32),
            pltpu.VMEM((HPG, 2 * SPAN, HD), f32),
            pltpu.VMEM((HPG, 2 * SPAN, HD), f32),
            pltpu.VMEM((HPG, SPAN, HD), bf),
            pltpu.VMEM((HPG, 8, HD), f32),
            pltpu.VMEM((HPG, SPAN, HD), bf),
            pltpu.VMEM((HPG, 8, HD), f32),
            pltpu.VMEM((SPAN, WIDTH), bf),
            dma((5, NU)), dma((5, NU)), dma((5,)),
            dma((2, 2, HALF, HPG)), dma((2, 2, HALF, HPG)),
            dma((2, NZ, HPG)), dma((2, NZ, HPG)),
            dma((2,)), dma((2, HPG)), dma((2, HPG)),
            dma((HPG, NU)), dma((HPG, NU)), dma((HPG,)),
        ],
        compiler_params=pltpu.CompilerParams(
            collective_id=0, has_side_effects=True, vmem_limit_bytes=50 * 1024 * 1024
        ),
    )(query, key_fresh, value_fresh, key_stale, value_stale)


def solution(mesh):
    spec = P(("patch", "uly"), None)
    return jax.shard_map(
        shards, mesh=mesh, in_specs=(spec,) * 5, out_specs=spec, check_vma=False,
    )
```

```python
import functools
import math

import jax
import jax.numpy as jnp
from jax import lax
from jax.experimental import pallas as pl
from jax.experimental.pallas import tpu as pltpu
from jax.sharding import PartitionSpec as P

HD = 128
HPG = 3
WIDTH = HPG * HD
NU = 8
NZ = 8
HALF = NZ // 2
SLICE = 48
SPAN = NU * SLICE
MESH = pl.DeviceIdType.MESH
C2 = HD ** (-0.5) * math.log2(math.e)


def slot_of(d, s):
    if s == 0:
        return 0
    if s == HALF:
        return HALF
    return s if d == 0 else HALF + s


def reach(t, d):
    return HALF if t == d else HALF - 1


TOPS = -1e30
NT = (((1,), (1,)), ((), ()))

UNITS = (
    (0, 1), (0, 5), (1, 1), (1, 5), (0, 2), (0, 6), (1, 2), (1, 6), (0, 0), (1, 0), (0, 3), (0, 7),
    (2, 0), (1, 3), (1, 7), (2, 1), (2, 5), (0, 4), (1, 4), (2, 2), (2, 6), (2, 3), (2, 7), (2, 4),
)


def pick(table, i):
    value = jnp.int32(table[0])
    for j in range(1, len(table)):
        value = jnp.where(i == j, jnp.int32(table[j]), value)
    return value


def kernel(q_in, kf_in, vf_in, ks_in, vs_in, out_ref,
           qbuf, kfb, vfb, kbuf, vbuf, acc, mx, ls, obuf, sbuf, ob_in, sb_in, res,
           a2a_send, a2a_recv, ring_send, ring_recv, sib_send, sib_recv,
           qp_send, qp_recv, part_send, part_recv, out_sems):
    patch = lax.axis_index("patch")
    u = lax.axis_index("uly")
    z = patch // 4
    yh = (patch // 2) % 2
    c = patch % 2
    up = ((z + 1) % NZ) * 4 + yh * 2 + c
    down = ((z + NZ - 1) % NZ) * 4 + yh * 2 + c
    sib = z * 4 + yh * 2 + (1 - c)
    par = z * 4 + (1 - yh) * 2 + c
    own0 = pl.multiple_of(c * SPAN, SPAN)
    sib0 = pl.multiple_of((1 - c) * SPAN, SPAN)
    crow = pl.ds(own0, SPAN)
    orow = pl.ds(sib0, SPAN)
    arow = pl.ds(0, SPAN)
    brow = pl.ds(SPAN, SPAN)

    barrier = pltpu.get_barrier_semaphore()
    for o in range(1, NU):
        pl.semaphore_signal(barrier, inc=1, device_id=(patch, (u + o) % NU), device_id_type=MESH)
    for p in (up, down, sib, par):
        pl.semaphore_signal(barrier, inc=1, device_id=(p, u), device_id_type=MESH)
    mx[...] = jnp.full_like(mx, TOPS)
    ls[...] = jnp.zeros_like(ls)
    acc[...] = jnp.zeros_like(acc)
    for h in range(HPG):
        sbuf[h] = jnp.zeros((8, HD), jnp.float32)
    pl.semaphore_wait(barrier, NU - 1 + 4)

    def cols(h):
        return pl.ds(pl.multiple_of(h * HD, HD), HD)

    def bytes_of(ref, sem):
        return pltpu.make_async_copy(ref, ref, sem)

    own_rows = pl.ds(pl.multiple_of(u * SLICE, SLICE), SLICE)
    own_place = pl.ds(pl.multiple_of(c * SPAN + u * SLICE, SLICE), SLICE)

    def spread(src, dst, first, width, k, r):
        for o in range(1, NU):
            peer = (u + o) % NU
            pltpu.make_async_remote_copy(
                src_ref=src.at[:, pl.ds(pl.multiple_of(peer * WIDTH + first, HD), width)], dst_ref=dst,
                send_sem=a2a_send.at[k], recv_sem=a2a_recv.at[r], device_id=(patch, peer), device_id_type=MESH).start()
        pltpu.make_async_copy(
            src.at[:, pl.ds(pl.multiple_of(u * WIDTH + first, HD), width)], dst, a2a_recv.at[r]).start()

    def spread_stale(h):
        spread(ks_in, kbuf.at[0, own_place, cols(h)], h * HD, HD, 0, h)
        spread(vs_in, vbuf.at[0, own_place, cols(h)], h * HD, HD, 0, h)

    spread_stale(0)
    spread_stale(1)
    spread(q_in, qbuf.at[own_rows], 0, WIDTH, 1, HPG)
    spread_stale(2)
    spread(kf_in, kfb.at[own_rows], 0, WIDTH, 2, HPG + 1)
    spread(vf_in, vfb.at[own_rows], 0, WIDTH, 2, HPG + 1)

    bufs = (kbuf, vbuf)

    def ring(t, d, s, h):
        return pltpu.make_async_remote_copy(
            src_ref=bufs[t].at[slot_of(d, s - 1), crow, cols(h)],
            dst_ref=bufs[t].at[slot_of(d, s), crow, cols(h)],
            send_sem=ring_send.at[0], recv_sem=ring_recv.at[t, d, s - 1, h],
            device_id=(up if d == 0 else down, u), device_id_type=MESH)

    def to_sib(t, slot, h):
        pltpu.make_async_remote_copy(
            src_ref=bufs[t].at[slot, crow, cols(h)], dst_ref=bufs[t].at[slot, crow, cols(h)],
            send_sem=sib_send.at[0], recv_sem=sib_recv.at[slot, h],
            device_id=(sib, u), device_id_type=MESH).start()

    def own_stale(h):
        bytes_of(kbuf.at[0, :, cols(h)], a2a_recv.at[h]).wait()

    def inject(h):
        for t in range(2):
            for d in range(2):
                ring(t, d, 1, h).start()

    def own_to_sib(h):
        for t in range(2):
            to_sib(t, 0, h)

    def arrive(h, s):
        for t in range(2):
            for d in range(2):
                if s > reach(t, d):
                    continue
                ring(t, d, s, h).wait_recv()
                if s < reach(t, d):
                    ring(t, d, s + 1, h).start()
                to_sib(t, slot_of(d, s), h)

    def q_par(h):
        return pltpu.make_async_remote_copy(
            src_ref=qbuf.at[arow, cols(h)], dst_ref=qbuf.at[brow, cols(h)],
            send_sem=qp_send.at[0], recv_sem=qp_recv.at[h], device_id=(par, u), device_id_type=MESH)

    def attend(h, r, k, v):
        s = lax.dot_general(qbuf[r, cols(h)], k, NT, preferred_element_type=jnp.float32) * C2
        m_old = mx[h, r, :]
        m_new = jnp.maximum(m_old, jnp.max(s, axis=1, keepdims=True))
        parts = [jnp.exp2(s[:, j * HD:(j + 1) * HD] - m_new) for j in range(k.shape[0] // HD)]
        tot = parts[0]
        for part in parts[1:]:
            tot = tot + part
        w = jnp.concatenate([part.astype(jnp.bfloat16) for part in parts], axis=1)
        pv = jnp.dot(w, v, preferred_element_type=jnp.float32)
        alpha = jnp.exp2(m_old - m_new)
        mx[h, r, :] = m_new
        ls[h, r, :] = ls[h, r, :] * alpha + tot
        acc[h, r, :] = acc[h, r, :] * alpha + pv

    def part_o(h):
        return pltpu.make_async_remote_copy(
            src_ref=obuf.at[h], dst_ref=ob_in.at[h], send_sem=part_send.at[0], recv_sem=part_recv.at[0, h],
            device_id=(par, u), device_id_type=MESH)

    def part_s(h):
        return pltpu.make_async_remote_copy(
            src_ref=sbuf.at[h], dst_ref=sb_in.at[h], send_sem=part_send.at[1], recv_sem=part_recv.at[1, h],
            device_id=(par, u), device_id_type=MESH)

    def give(h):
        total = jnp.sum(ls[h, brow, :], axis=1, keepdims=True)
        obuf[h] = (acc[h, brow, :] / total).astype(jnp.bfloat16)
        lse = mx[h, brow, :] + jnp.log2(total)
        for i in range(SPAN // HD):
            sbuf[h, i:i + 1, :] = jnp.transpose(lse[i * HD:(i + 1) * HD, :])[0:1, :]
        part_o(h).start()
        part_s(h).start()

    def merge(h):
        part_o(h).wait_recv()
        part_s(h).wait_recv()
        for i in range(SPAN // HD):
            r = pl.ds(i * HD, HD)
            tot_a = jnp.sum(ls[h, r, :], axis=1, keepdims=True)
            lse_a = mx[h, r, :] + jnp.log2(tot_a)
            lse_b = jnp.transpose(jnp.broadcast_to(sb_in[h, i:i + 1, :], (HD, HD)))
            peak = jnp.maximum(lse_a, lse_b)
            wa = jnp.exp2(lse_a - peak)
            wb = jnp.exp2(lse_b - peak)
            both = (wa / tot_a) * acc[h, r, :] + wb * ob_in[h, r, :].astype(jnp.float32)
            res[r, cols(h)] = (both / (wa + wb)).astype(jnp.bfloat16)
        land = out_ref.at[:, pl.ds(pl.multiple_of(u * WIDTH + h * HD, HD), HD)]
        for o in range(1, NU):
            peer = (u + o) % NU
            pltpu.make_async_remote_copy(
                src_ref=res.at[pl.ds(pl.multiple_of(peer * SLICE, SLICE), SLICE), cols(h)], dst_ref=land,
                send_sem=out_sems.at[0], recv_sem=out_sems.at[1],
                device_id=(patch, peer), device_id_type=MESH).start()
        pltpu.make_async_copy(res.at[own_rows, cols(h)], land, out_sems.at[1]).start()

    own_stale(0)
    inject(0)
    own_to_sib(0)
    own_stale(1)
    inject(1)
    own_to_sib(1)
    arrive(0, 1)
    bytes_of(qbuf.at[arow], a2a_recv.at[HPG]).wait()
    for h in range(HPG):
        q_par(h).start()
    own_stale(2)
    own_to_sib(2)
    arrive(1, 1)
    q_par(0).wait_recv()

    def fresh():
        bytes_of(kbuf.at[0], a2a_recv.at[HPG + 1]).wait()

    def second():
        arrive(1, 2)
        inject(2)

    before = {
        2: lambda: (arrive(0, 2), q_par(1).wait_recv()),
        6: second,
        8: fresh,
        10: lambda: arrive(0, 3),
        12: lambda: q_par(2).wait_recv(),
        13: lambda: arrive(1, 3),
        15: lambda: arrive(2, 1),
        17: lambda: arrive(0, 4),
        18: lambda: (give(0), arrive(1, 4)),
        19: lambda: (give(1), arrive(2, 2)),
        21: lambda: (merge(0), arrive(2, 3)),
        23: lambda: arrive(2, 4),
    }

    def unit(i, carry):
        for j, event in before.items():
            pl.when(i == j)(lambda event=event: (event(), None)[1])
        h = pick([a for a, _ in UNITS], i)
        slot = pick([b for _, b in UNITS], i)
        bytes_of(kbuf.at[slot, :, cols(h)], sib_recv.at[slot, h]).wait()

        @pl.when(slot != 0)
        def _():
            attend(h, pl.ds(0, 2 * SPAN), kbuf[slot, :, cols(h)], vbuf[slot, :, cols(h)])

        @pl.when(slot == 0)
        def _():
            attend(h, pl.ds(0, 2 * SPAN), kbuf[0, orow, cols(h)], vbuf[0, orow, cols(h)])
            attend(h, arow, kfb[:, cols(h)], vfb[:, cols(h)])
            attend(h, brow, kbuf[0, crow, cols(h)], vbuf[0, crow, cols(h)])
        return carry

    lax.fori_loop(0, len(UNITS), unit, 0)
    give(2)
    merge(1)
    merge(2)

    bytes_of(res, out_sems.at[1]).wait()
    bytes_of(res.at[pl.ds(0, (NU - 1) * SLICE)], out_sems.at[0]).wait()
    bytes_of(obuf, part_send.at[0]).wait()
    bytes_of(sbuf, part_send.at[1]).wait()
    bytes_of(qbuf.at[arow], qp_send.at[0]).wait()
    bytes_of(kbuf, sib_send.at[0]).wait()
    bytes_of(kbuf.at[pl.ds(0, NZ - 1)], ring_send.at[0]).wait()
    bytes_of(kbuf.at[0, pl.ds(0, 2 * (NU - 1) * SLICE)], a2a_send.at[0]).wait()
    bytes_of(qbuf.at[pl.ds(0, (NU - 1) * SLICE)], a2a_send.at[1]).wait()
    bytes_of(kbuf.at[0, pl.ds(0, 2 * (NU - 1) * SLICE)], a2a_send.at[2]).wait()


def shards(query, key_fresh, value_fresh, key_stale, value_stale):
    bf, f32 = jnp.bfloat16, jnp.float32
    dma = pltpu.SemaphoreType.DMA
    return pl.pallas_call(
        kernel,
        out_shape=jax.ShapeDtypeStruct(query.shape, bf),
        in_specs=[pl.BlockSpec(memory_space=pl.ANY)] * 5,
        out_specs=pl.BlockSpec(memory_space=pl.ANY),
        scratch_shapes=[
            pltpu.VMEM((2 * SPAN, WIDTH), bf),
            pltpu.VMEM((SPAN, WIDTH), bf),
            pltpu.VMEM((SPAN, WIDTH), bf),
            pltpu.VMEM((NZ, 2 * SPAN, WIDTH), bf),
            pltpu.VMEM((NZ, 2 * SPAN, WIDTH), bf),
            pltpu.VMEM((HPG, 2 * SPAN, HD), f32),
            pltpu.VMEM((HPG, 2 * SPAN, HD), f32),
            pltpu.VMEM((HPG, 2 * SPAN, HD), f32),
            pltpu.VMEM((HPG, SPAN, HD), bf),
            pltpu.VMEM((HPG, 8, HD), f32),
            pltpu.VMEM((HPG, SPAN, HD), bf),
            pltpu.VMEM((HPG, 8, HD), f32),
            pltpu.VMEM((SPAN, WIDTH), bf),
            dma((3,)), dma((HPG + 2,)),
            dma((1,)), dma((2, 2, HALF, HPG)),
            dma((1,)), dma((NZ, HPG)),
            dma((1,)), dma((HPG,)),
            dma((2,)), dma((2, HPG)), dma((2,)),
        ],
        compiler_params=pltpu.CompilerParams(
            collective_id=0, has_side_effects=True, vmem_limit_bytes=62 * 1024 * 1024
        ),
    )(query, key_fresh, value_fresh, key_stale, value_stale)


def solution(mesh):
    spec = P(("patch", "uly"), None)
    return jax.shard_map(
        shards, mesh=mesh, in_specs=(spec,) * 5, out_specs=spec, check_vma=False,
    )
```

```python
import functools
import math

import jax
import jax.numpy as jnp
from jax import lax
from jax.experimental import pallas as pl
from jax.experimental.pallas import tpu as pltpu
from jax.sharding import PartitionSpec as P

HD = 128
HPG = 3
WIDTH = HPG * HD
NU = 8
NZ = 8
HALF = NZ // 2
SLICE = 48
SPAN = NU * SLICE
MESH = pl.DeviceIdType.MESH
C2 = HD ** (-0.5) * math.log2(math.e)


def slot_of(d, s):
    if s == 0:
        return 0
    if s == HALF:
        return HALF
    return s if d == 0 else HALF + s


def reach(t, d):
    return HALF if t == d else HALF - 1


TOPS = -1e30
NT = (((1,), (1,)), ((), ()))

PAIRS = (
    ((0, 1), (0, 5)), ((1, 1), (1, 5)), ((0, 2), (0, 6)), ((1, 2), (1, 6)), ((0, 3), (0, 7)),
    ((1, 3), (1, 7)), ((2, 1), (0, 4)), ((2, 5), (1, 4)), ((2, 2), (2, 6)), ((2, 3), (2, 7)),
)
CHUNK = 256


def pick(table, i):
    value = jnp.int32(table[0])
    for j in range(1, len(table)):
        value = jnp.where(i == j, jnp.int32(table[j]), value)
    return value


def kernel(q_in, kf_in, vf_in, ks_in, vs_in, out_ref,
           qbuf, kfb, vfb, kbuf, vbuf, acc, mx, ls, obuf, sbuf, ob_in, sb_in, res,
           a2a_send, a2a_recv, ring_send, ring_recv, sib_send, sib_recv,
           qp_send, qp_recv, part_send, part_recv, out_sems):
    patch = lax.axis_index("patch")
    u = lax.axis_index("uly")
    z = patch // 4
    yh = (patch // 2) % 2
    c = patch % 2
    up = ((z + 1) % NZ) * 4 + yh * 2 + c
    down = ((z + NZ - 1) % NZ) * 4 + yh * 2 + c
    sib = z * 4 + yh * 2 + (1 - c)
    par = z * 4 + (1 - yh) * 2 + c
    own0 = pl.multiple_of(c * SPAN, SPAN)
    sib0 = pl.multiple_of((1 - c) * SPAN, SPAN)
    crow = pl.ds(own0, SPAN)
    orow = pl.ds(sib0, SPAN)
    arow = pl.ds(0, SPAN)
    brow = pl.ds(SPAN, SPAN)

    barrier = pltpu.get_barrier_semaphore()
    for o in range(1, NU):
        pl.semaphore_signal(barrier, inc=1, device_id=(patch, (u + o) % NU), device_id_type=MESH)
    for p in (up, down, sib, par):
        pl.semaphore_signal(barrier, inc=1, device_id=(p, u), device_id_type=MESH)
    mx[...] = jnp.full_like(mx, TOPS)
    ls[...] = jnp.zeros_like(ls)
    acc[...] = jnp.zeros_like(acc)
    for h in range(HPG):
        sbuf[h] = jnp.zeros((8, HD), jnp.float32)
    pl.semaphore_wait(barrier, NU - 1 + 4)

    def cols(h):
        return pl.ds(pl.multiple_of(h * HD, HD), HD)

    def bytes_of(ref, sem):
        return pltpu.make_async_copy(ref, ref, sem)

    own_rows = pl.ds(pl.multiple_of(u * SLICE, SLICE), SLICE)
    own_place = pl.ds(pl.multiple_of(c * SPAN + u * SLICE, SLICE), SLICE)

    def spread(src, dst, first, width, k, r):
        for o in range(1, NU):
            peer = (u + o) % NU
            pltpu.make_async_remote_copy(
                src_ref=src.at[:, pl.ds(pl.multiple_of(peer * WIDTH + first, HD), width)], dst_ref=dst,
                send_sem=a2a_send.at[k], recv_sem=a2a_recv.at[r], device_id=(patch, peer), device_id_type=MESH).start()
        pltpu.make_async_copy(
            src.at[:, pl.ds(pl.multiple_of(u * WIDTH + first, HD), width)], dst, a2a_recv.at[r]).start()

    def spread_stale(h):
        spread(ks_in, kbuf.at[0, own_place, cols(h)], h * HD, HD, 0, h)
        spread(vs_in, vbuf.at[0, own_place, cols(h)], h * HD, HD, 0, HPG + h)

    spread_stale(0)
    spread_stale(1)
    spread(q_in, qbuf.at[own_rows], 0, WIDTH, 1, 2 * HPG)
    spread_stale(2)
    spread(kf_in, kfb.at[own_rows], 0, WIDTH, 2, 2 * HPG + 1)
    spread(vf_in, vfb.at[own_rows], 0, WIDTH, 2, 2 * HPG + 1)

    bufs = (kbuf, vbuf)

    def ring(t, d, s, h):
        return pltpu.make_async_remote_copy(
            src_ref=bufs[t].at[slot_of(d, s - 1), crow, cols(h)],
            dst_ref=bufs[t].at[slot_of(d, s), crow, cols(h)],
            send_sem=ring_send.at[0], recv_sem=ring_recv.at[t, d, s - 1, h],
            device_id=(up if d == 0 else down, u), device_id_type=MESH)

    def to_sib(t, slot, h):
        pltpu.make_async_remote_copy(
            src_ref=bufs[t].at[slot, crow, cols(h)], dst_ref=bufs[t].at[slot, crow, cols(h)],
            send_sem=sib_send.at[0], recv_sem=sib_recv.at[slot, h],
            device_id=(sib, u), device_id_type=MESH).start()

    def own_stale(h, t):
        bytes_of(bufs[t].at[0, crow, cols(h)], a2a_recv.at[t * HPG + h]).wait()

    def inject(h, t):
        for d in range(2):
            ring(t, d, 1, h).start()

    def begin(h):
        for t in range(2):
            own_stale(h, t)
            inject(h, t)
            to_sib(t, 0, h)

    def arrive(h, s):
        for t in range(2):
            for d in range(2):
                if s > reach(t, d):
                    continue
                ring(t, d, s, h).wait_recv()
                if s < reach(t, d):
                    ring(t, d, s + 1, h).start()
                to_sib(t, slot_of(d, s), h)

    def q_par(h):
        return pltpu.make_async_remote_copy(
            src_ref=qbuf.at[arow, cols(h)], dst_ref=qbuf.at[brow, cols(h)],
            send_sem=qp_send.at[0], recv_sem=qp_recv.at[h], device_id=(par, u), device_id_type=MESH)

    def attend(h, r, k, v):
        n = k.shape[0]
        step = CHUNK if n % CHUNK == 0 else n
        for first in range(0, n, step):
            part_rows = pl.ds(first, step)
            s = lax.dot_general(qbuf[r, cols(h)], k[part_rows, :], NT, preferred_element_type=jnp.float32)
            m_old = mx[h, r, :]
            m_new = jnp.maximum(m_old, jnp.max(s, axis=1, keepdims=True))
            parts = [jnp.exp2((s[:, j * HD:(j + 1) * HD] - m_new) * C2) for j in range(step // HD)]
            tot = parts[0]
            for part in parts[1:]:
                tot = tot + part
            w = jnp.concatenate([part.astype(jnp.bfloat16) for part in parts], axis=1)
            pv = jnp.dot(w, v[part_rows, :], preferred_element_type=jnp.float32)
            alpha = jnp.exp2((m_old - m_new) * C2)
            mx[h, r, :] = m_new
            ls[h, r, :] = ls[h, r, :] * alpha + tot
            acc[h, r, :] = acc[h, r, :] * alpha + pv

    def block(h, slot, r):
        attend(h, r, kbuf.at[slot, :, cols(h)], vbuf.at[slot, :, cols(h)])

    def part_o(h):
        return pltpu.make_async_remote_copy(
            src_ref=obuf.at[h], dst_ref=ob_in.at[h], send_sem=part_send.at[0], recv_sem=part_recv.at[0, h],
            device_id=(par, u), device_id_type=MESH)

    def part_s(h):
        return pltpu.make_async_remote_copy(
            src_ref=sbuf.at[h], dst_ref=sb_in.at[h], send_sem=part_send.at[1], recv_sem=part_recv.at[1, h],
            device_id=(par, u), device_id_type=MESH)

    def give(h):
        total = jnp.sum(ls[h, brow, :], axis=1, keepdims=True)
        obuf[h] = (acc[h, brow, :] / total).astype(jnp.bfloat16)
        lse = mx[h, brow, :] * C2 + jnp.log2(total)
        for i in range(SPAN // HD):
            sbuf[h, i:i + 1, :] = jnp.transpose(lse[i * HD:(i + 1) * HD, :])[0:1, :]
        part_o(h).start()
        part_s(h).start()

    def merge(h):
        part_o(h).wait_recv()
        part_s(h).wait_recv()
        for i in range(SPAN // HD):
            r = pl.ds(i * HD, HD)
            tot_a = jnp.sum(ls[h, r, :], axis=1, keepdims=True)
            lse_a = mx[h, r, :] * C2 + jnp.log2(tot_a)
            lse_b = jnp.transpose(jnp.broadcast_to(sb_in[h, i:i + 1, :], (HD, HD)))
            peak = jnp.maximum(lse_a, lse_b)
            wa = jnp.exp2(lse_a - peak)
            wb = jnp.exp2(lse_b - peak)
            both = (wa / tot_a) * acc[h, r, :] + wb * ob_in[h, r, :].astype(jnp.float32)
            res[r, cols(h)] = (both / (wa + wb)).astype(jnp.bfloat16)
        land = out_ref.at[:, pl.ds(pl.multiple_of(u * WIDTH + h * HD, HD), HD)]
        for o in range(1, NU):
            peer = (u + o) % NU
            pltpu.make_async_remote_copy(
                src_ref=res.at[pl.ds(pl.multiple_of(peer * SLICE, SLICE), SLICE), cols(h)], dst_ref=land,
                send_sem=out_sems.at[0], recv_sem=out_sems.at[1],
                device_id=(patch, peer), device_id_type=MESH).start()
        pltpu.make_async_copy(res.at[own_rows, cols(h)], land, out_sems.at[1]).start()

    begin(0)
    begin(1)
    arrive(0, 1)
    bytes_of(qbuf.at[arow], a2a_recv.at[2 * HPG]).wait()
    for h in range(HPG):
        q_par(h).start()
    for t in range(2):
        own_stale(2, t)
        to_sib(t, 0, 2)
    arrive(1, 1)
    q_par(0).wait_recv()

    def wait_sib(h, slot):
        bytes_of(kbuf.at[slot, :, cols(h)], sib_recv.at[slot, h]).wait()

    def own_chip():
        bytes_of(kbuf.at[0], a2a_recv.at[2 * HPG + 1]).wait()
        q_par(2).wait_recv()

        def head(h, carry):
            wait_sib(h, 0)
            attend(h, pl.ds(0, 2 * SPAN), kbuf.at[0, orow, cols(h)], vbuf.at[0, orow, cols(h)])
            attend(h, arow, kfb.at[:, cols(h)], vfb.at[:, cols(h)])
            attend(h, brow, kbuf.at[0, crow, cols(h)], vbuf.at[0, crow, cols(h)])
            return carry

        lax.fori_loop(0, HPG, head, 0)

    def later():
        arrive(1, 2)
        for t in range(2):
            inject(2, t)

    before = {
        1: lambda: (arrive(0, 2), q_par(1).wait_recv()),
        3: later,
        4: lambda: (own_chip(), arrive(0, 3)),
        5: lambda: arrive(1, 3),
        6: lambda: (arrive(2, 1), arrive(0, 4)),
        7: lambda: (give(0), arrive(1, 4)),
        8: lambda: (give(1), arrive(2, 2)),
        9: lambda: (arrive(2, 3), merge(0)),
    }

    def pair(i, carry):
        for j, event in before.items():
            pl.when(i == j)(lambda event=event: (event(), None)[1])
        both = [(pick([p[g][0] for p in PAIRS], i), pick([p[g][1] for p in PAIRS], i)) for g in range(2)]
        for h, slot in both:
            wait_sib(h, slot)
        for h, slot in both:
            block(h, slot, pl.ds(0, 2 * SPAN))
        return carry

    lax.fori_loop(0, len(PAIRS), pair, 0)
    arrive(2, HALF)
    wait_sib(2, HALF)
    block(2, HALF, brow)
    give(2)
    block(2, HALF, arow)
    merge(1)
    merge(2)

    bytes_of(res, out_sems.at[1]).wait()
    bytes_of(res.at[pl.ds(0, (NU - 1) * SLICE)], out_sems.at[0]).wait()
    bytes_of(obuf, part_send.at[0]).wait()
    bytes_of(sbuf, part_send.at[1]).wait()
    bytes_of(qbuf.at[arow], qp_send.at[0]).wait()
    bytes_of(kbuf, sib_send.at[0]).wait()
    bytes_of(kbuf.at[pl.ds(0, NZ - 1)], ring_send.at[0]).wait()
    bytes_of(kbuf.at[0, pl.ds(0, 2 * (NU - 1) * SLICE)], a2a_send.at[0]).wait()
    bytes_of(qbuf.at[pl.ds(0, (NU - 1) * SLICE)], a2a_send.at[1]).wait()
    bytes_of(kbuf.at[0, pl.ds(0, 2 * (NU - 1) * SLICE)], a2a_send.at[2]).wait()


def shards(query, key_fresh, value_fresh, key_stale, value_stale):
    bf, f32 = jnp.bfloat16, jnp.float32
    dma = pltpu.SemaphoreType.DMA
    return pl.pallas_call(
        kernel,
        out_shape=jax.ShapeDtypeStruct(query.shape, bf),
        in_specs=[pl.BlockSpec(memory_space=pl.ANY)] * 5,
        out_specs=pl.BlockSpec(memory_space=pl.ANY),
        scratch_shapes=[
            pltpu.VMEM((2 * SPAN, WIDTH), bf),
            pltpu.VMEM((SPAN, WIDTH), bf),
            pltpu.VMEM((SPAN, WIDTH), bf),
            pltpu.VMEM((NZ, 2 * SPAN, WIDTH), bf),
            pltpu.VMEM((NZ, 2 * SPAN, WIDTH), bf),
            pltpu.VMEM((HPG, 2 * SPAN, HD), f32),
            pltpu.VMEM((HPG, 2 * SPAN, HD), f32),
            pltpu.VMEM((HPG, 2 * SPAN, HD), f32),
            pltpu.VMEM((HPG, SPAN, HD), bf),
            pltpu.VMEM((HPG, 8, HD), f32),
            pltpu.VMEM((HPG, SPAN, HD), bf),
            pltpu.VMEM((HPG, 8, HD), f32),
            pltpu.VMEM((SPAN, WIDTH), bf),
            dma((3,)), dma((2 * HPG + 2,)),
            dma((1,)), dma((2, 2, HALF, HPG)),
            dma((1,)), dma((NZ, HPG)),
            dma((1,)), dma((HPG,)),
            dma((2,)), dma((2, HPG)), dma((2,)),
        ],
        compiler_params=pltpu.CompilerParams(
            collective_id=0, has_side_effects=True, vmem_limit_bytes=62 * 1024 * 1024
        ),
    )(query, key_fresh, value_fresh, key_stale, value_stale)


def solution(mesh):
    spec = P(("patch", "uly"), None)
    return jax.shard_map(
        shards, mesh=mesh, in_specs=(spec,) * 5, out_specs=spec, check_vma=False,
    )
```

```python
import functools
import math

import jax
import jax.numpy as jnp
from jax import lax
from jax.experimental import pallas as pl
from jax.experimental.pallas import tpu as pltpu
from jax.sharding import PartitionSpec as P

HD = 128
HPG = 3
WIDTH = HPG * HD
NU = 8
NZ = 8
HALF = NZ // 2
SLICE = 48
SPAN = NU * SLICE
TAIL = 16
MESH = pl.DeviceIdType.MESH
C2 = HD ** (-0.5) * math.log2(math.e)


def slot_of(d, s):
    if s == 0:
        return 0
    if s == HALF:
        return HALF
    return s if d == 0 else HALF + s


def reach(t, d):
    return HALF if t == d else HALF - 1


TOPS = -1e30
NT = (((1,), (1,)), ((), ()))

PAIRS = (
    ((0, 1), (0, 5)), ((1, 1), (1, 5)), ((0, 2), (0, 6)), ((1, 2), (1, 6)), ((0, 3), (0, 7)),
    ((1, 3), (1, 7)), ((2, 1), (0, 4)), ((2, 5), (1, 4)), ((2, 2), (2, 6)), ((2, 3), (2, 7)),
)
CHUNK = 256


def pick(table, i):
    value = jnp.int32(table[0])
    for j in range(1, len(table)):
        value = jnp.where(i == j, jnp.int32(table[j]), value)
    return value


def kernel(q_in, kf_in, vf_in, ks_in, vs_in, out_ref,
           qbuf, kfb, vfb, kbuf, vbuf, acc, mx, ls, gives, takes,
           a2a_send, a2a_recv, ring_send, ring_recv, sib_send, sib_recv,
           qp_send, qp_recv, give_send, take_recv):
    patch = lax.axis_index("patch")
    u = lax.axis_index("uly")
    z = patch // 4
    yh = (patch // 2) % 2
    c = patch % 2
    up = ((z + 1) % NZ) * 4 + yh * 2 + c
    down = ((z + NZ - 1) % NZ) * 4 + yh * 2 + c
    sib = z * 4 + yh * 2 + (1 - c)
    par = z * 4 + (1 - yh) * 2 + c
    own0 = pl.multiple_of(c * SPAN, SPAN)
    sib0 = pl.multiple_of((1 - c) * SPAN, SPAN)
    crow = pl.ds(own0, SPAN)
    orow = pl.ds(sib0, SPAN)
    arow = pl.ds(0, SPAN)
    brow = pl.ds(SPAN, SPAN)

    barrier = pltpu.get_barrier_semaphore()
    for o in range(1, NU):
        pl.semaphore_signal(barrier, inc=1, device_id=(patch, (u + o) % NU), device_id_type=MESH)
    for p in (up, down, sib):
        pl.semaphore_signal(barrier, inc=1, device_id=(p, u), device_id_type=MESH)
    for o in range(NU):
        pl.semaphore_signal(barrier, inc=1, device_id=(par, (u + o) % NU), device_id_type=MESH)
    mx[...] = jnp.full_like(mx, TOPS)
    ls[...] = jnp.zeros_like(ls)
    acc[...] = jnp.zeros_like(acc)
    pl.semaphore_wait(barrier, 2 * NU - 1 + 3)

    def cols(h):
        return pl.ds(pl.multiple_of(h * HD, HD), HD)

    def bytes_of(ref, sem):
        return pltpu.make_async_copy(ref, ref, sem)

    own_rows = pl.ds(pl.multiple_of(u * SLICE, SLICE), SLICE)
    own_place = pl.ds(pl.multiple_of(c * SPAN + u * SLICE, SLICE), SLICE)

    def spread(src, dst, first, width, k, r):
        for o in range(1, NU):
            peer = (u + o) % NU
            pltpu.make_async_remote_copy(
                src_ref=src.at[:, pl.ds(pl.multiple_of(peer * WIDTH + first, HD), width)], dst_ref=dst,
                send_sem=a2a_send.at[k], recv_sem=a2a_recv.at[r], device_id=(patch, peer), device_id_type=MESH).start()
        pltpu.make_async_copy(
            src.at[:, pl.ds(pl.multiple_of(u * WIDTH + first, HD), width)], dst, a2a_recv.at[r]).start()

    def spread_stale(h):
        spread(ks_in, kbuf.at[0, own_place, cols(h)], h * HD, HD, 0, h)
        spread(vs_in, vbuf.at[0, own_place, cols(h)], h * HD, HD, 0, HPG + h)

    spread_stale(0)
    spread_stale(1)
    spread(q_in, qbuf.at[own_rows], 0, WIDTH, 1, 2 * HPG)
    spread_stale(2)
    spread(kf_in, kfb.at[own_rows], 0, WIDTH, 2, 2 * HPG + 1)
    spread(vf_in, vfb.at[own_rows], 0, WIDTH, 2, 2 * HPG + 1)

    bufs = (kbuf, vbuf)

    def ring(t, d, s, h):
        return pltpu.make_async_remote_copy(
            src_ref=bufs[t].at[slot_of(d, s - 1), crow, cols(h)],
            dst_ref=bufs[t].at[slot_of(d, s), crow, cols(h)],
            send_sem=ring_send.at[0], recv_sem=ring_recv.at[t, d, s - 1, h],
            device_id=(up if d == 0 else down, u), device_id_type=MESH)

    def to_sib(t, slot, h):
        pltpu.make_async_remote_copy(
            src_ref=bufs[t].at[slot, crow, cols(h)], dst_ref=bufs[t].at[slot, crow, cols(h)],
            send_sem=sib_send.at[0], recv_sem=sib_recv.at[slot, h],
            device_id=(sib, u), device_id_type=MESH).start()

    def own_stale(h, t):
        bytes_of(bufs[t].at[0, crow, cols(h)], a2a_recv.at[t * HPG + h]).wait()

    def inject(h, t):
        for d in range(2):
            ring(t, d, 1, h).start()

    def begin(h):
        for t in range(2):
            own_stale(h, t)
            inject(h, t)
            to_sib(t, 0, h)

    def arrive(h, s):
        for t in range(2):
            for d in range(2):
                if s > reach(t, d):
                    continue
                ring(t, d, s, h).wait_recv()
                if s < reach(t, d):
                    ring(t, d, s + 1, h).start()
                to_sib(t, slot_of(d, s), h)

    def q_par(h):
        return pltpu.make_async_remote_copy(
            src_ref=qbuf.at[arow, cols(h)], dst_ref=qbuf.at[brow, cols(h)],
            send_sem=qp_send.at[0], recv_sem=qp_recv.at[h], device_id=(par, u), device_id_type=MESH)

    def attend(h, r, k, v):
        n = k.shape[0]
        step = CHUNK if n % CHUNK == 0 else n
        for first in range(0, n, step):
            part_rows = pl.ds(first, step)
            s = lax.dot_general(qbuf[r, cols(h)], k[part_rows, :], NT, preferred_element_type=jnp.float32)
            m_old = mx[h, r, :]
            m_new = jnp.maximum(m_old, jnp.max(s, axis=1, keepdims=True))
            parts = [jnp.exp2((s[:, j * HD:(j + 1) * HD] - m_new) * C2) for j in range(step // HD)]
            tot = parts[0]
            for part in parts[1:]:
                tot = tot + part
            w = jnp.concatenate([part.astype(jnp.bfloat16) for part in parts], axis=1)
            pv = jnp.dot(w, v[part_rows, :], preferred_element_type=jnp.float32)
            alpha = jnp.exp2((m_old - m_new) * C2)
            mx[h, r, :] = m_new
            ls[h, r, :] = ls[h, r, :] * alpha + tot
            acc[h, r, :] = acc[h, r, :] * alpha + pv

    def block(h, slot, r):
        attend(h, r, kbuf.at[slot, :, cols(h)], vbuf.at[slot, :, cols(h)])

    tail_row = lax.broadcasted_iota(jnp.int32, (TAIL, HD), 0)
    diagonal = lax.broadcasted_iota(jnp.int32, (SLICE, HD), 0) == lax.broadcasted_iota(jnp.int32, (SLICE, HD), 1)

    def give(h, side):
        r = pl.ds(side * SPAN, SPAN)
        total = jnp.sum(ls[h, r, :], axis=1, keepdims=True)
        part = (acc[h, r, :] / total).astype(jnp.bfloat16)
        lse = mx[h, r, :] * C2 + jnp.log2(total)
        for p in range(NU):
            rows = slice(p * SLICE, (p + 1) * SLICE)
            line = jnp.sum(jnp.where(diagonal, lse[rows], 0.0), axis=0, keepdims=True)
            high = line.astype(jnp.bfloat16).astype(jnp.float32)
            middle = (line - high).astype(jnp.bfloat16).astype(jnp.float32)
            low = line - high - middle
            end = jnp.where(tail_row == 0, high, jnp.where(tail_row == 1, middle, jnp.where(tail_row == 2, low, 0.0)))
            gives[side, h, p, 0:SLICE, :] = part[rows]
            gives[side, h, p, SLICE:SLICE + TAIL, :] = end.astype(jnp.bfloat16)
        for o in range(NU):
            peer = (u + o) % NU
            if side == 0 and o == 0:
                pltpu.make_async_copy(gives.at[0, h, u], takes.at[0, h, u], take_recv.at[0, h]).start()
            else:
                pltpu.make_async_remote_copy(
                    src_ref=gives.at[side, h, peer], dst_ref=takes.at[side, h, u],
                    send_sem=give_send.at[side], recv_sem=take_recv.at[side, h],
                    device_id=(patch if side == 0 else par, peer), device_id_type=MESH).start()

    def merge(h):
        for side in range(2):
            bytes_of(takes.at[side, h], take_recv.at[side, h]).wait()
        for g in range(NU):
            sums, lses = [], []
            for side in range(2):
                sums.append(takes[side, h, g, 0:SLICE, :].astype(jnp.float32))
                end = takes[side, h, g, SLICE:SLICE + TAIL, :].astype(jnp.float32)
                line = jnp.sum(end, axis=0, keepdims=True)
                lses.append(jnp.sum(jnp.where(diagonal, line, 0.0), axis=1, keepdims=True))
            peak = jnp.maximum(lses[0], lses[1])
            wa = jnp.exp2(lses[0] - peak)
            wb = jnp.exp2(lses[1] - peak)
            both = (wa * sums[0] + wb * sums[1]) / (wa + wb)
            out_ref[:, (g * HPG + h) * HD:(g * HPG + h + 1) * HD] = both.astype(jnp.bfloat16)

    begin(0)
    begin(1)
    arrive(0, 1)
    bytes_of(qbuf.at[arow], a2a_recv.at[2 * HPG]).wait()
    for h in range(HPG):
        q_par(h).start()
    for t in range(2):
        own_stale(2, t)
        to_sib(t, 0, 2)
    arrive(1, 1)
    q_par(0).wait_recv()

    def wait_sib(h, slot):
        bytes_of(kbuf.at[slot, :, cols(h)], sib_recv.at[slot, h]).wait()

    def own_chip():
        bytes_of(kbuf.at[0], a2a_recv.at[2 * HPG + 1]).wait()
        q_par(2).wait_recv()

        def head(h, carry):
            wait_sib(h, 0)
            attend(h, pl.ds(0, 2 * SPAN), kbuf.at[0, orow, cols(h)], vbuf.at[0, orow, cols(h)])
            attend(h, arow, kfb.at[:, cols(h)], vfb.at[:, cols(h)])
            attend(h, brow, kbuf.at[0, crow, cols(h)], vbuf.at[0, crow, cols(h)])
            return carry

        lax.fori_loop(0, HPG, head, 0)

    def later():
        arrive(1, 2)
        for t in range(2):
            inject(2, t)

    before = {
        1: lambda: (arrive(0, 2), q_par(1).wait_recv()),
        3: later,
        4: lambda: (own_chip(), arrive(0, 3)),
        5: lambda: arrive(1, 3),
        6: lambda: (arrive(2, 1), arrive(0, 4)),
        7: lambda: (arrive(1, 4), give(0, 1), give(0, 0)),
        8: lambda: (give(1, 1), give(1, 0), arrive(2, 2)),
        9: lambda: (arrive(2, 3), merge(0)),
    }

    def pair(i, carry):
        for j, event in before.items():
            pl.when(i == j)(lambda event=event: (event(), None)[1])
        both = [(pick([p[g][0] for p in PAIRS], i), pick([p[g][1] for p in PAIRS], i)) for g in range(2)]
        for h, slot in both:
            wait_sib(h, slot)
        for h, slot in both:
            block(h, slot, pl.ds(0, 2 * SPAN))
        return carry

    lax.fori_loop(0, len(PAIRS), pair, 0)
    arrive(2, HALF)
    attend(2, pl.ds(0, 2 * SPAN), kbuf.at[HALF, crow, cols(2)], vbuf.at[HALF, crow, cols(2)])
    wait_sib(2, HALF)
    attend(2, brow, kbuf.at[HALF, orow, cols(2)], vbuf.at[HALF, orow, cols(2)])
    give(2, 1)
    attend(2, arow, kbuf.at[HALF, orow, cols(2)], vbuf.at[HALF, orow, cols(2)])
    give(2, 0)
    merge(1)
    merge(2)

    bytes_of(gives.at[0, :, pl.ds(0, NU - 1)], give_send.at[0]).wait()
    bytes_of(gives.at[1], give_send.at[1]).wait()
    bytes_of(qbuf.at[arow], qp_send.at[0]).wait()
    bytes_of(kbuf, sib_send.at[0]).wait()
    bytes_of(kbuf.at[pl.ds(0, NZ - 1)], ring_send.at[0]).wait()
    bytes_of(kbuf.at[0, pl.ds(0, 2 * (NU - 1) * SLICE)], a2a_send.at[0]).wait()
    bytes_of(qbuf.at[pl.ds(0, (NU - 1) * SLICE)], a2a_send.at[1]).wait()
    bytes_of(kbuf.at[0, pl.ds(0, 2 * (NU - 1) * SLICE)], a2a_send.at[2]).wait()


def shards(query, key_fresh, value_fresh, key_stale, value_stale):
    bf, f32 = jnp.bfloat16, jnp.float32
    dma = pltpu.SemaphoreType.DMA
    return pl.pallas_call(
        kernel,
        out_shape=jax.ShapeDtypeStruct(query.shape, bf),
        in_specs=[pl.BlockSpec(memory_space=pl.ANY)] * 5,
        out_specs=pl.BlockSpec(memory_space=pltpu.VMEM),
        scratch_shapes=[
            pltpu.VMEM((2 * SPAN, WIDTH), bf),
            pltpu.VMEM((SPAN, WIDTH), bf),
            pltpu.VMEM((SPAN, WIDTH), bf),
            pltpu.VMEM((NZ, 2 * SPAN, WIDTH), bf),
            pltpu.VMEM((NZ, 2 * SPAN, WIDTH), bf),
            pltpu.VMEM((HPG, 2 * SPAN, HD), f32),
            pltpu.VMEM((HPG, 2 * SPAN, HD), f32),
            pltpu.VMEM((HPG, 2 * SPAN, HD), f32),
            pltpu.VMEM((2, HPG, NU, SLICE + TAIL, HD), bf),
            pltpu.VMEM((2, HPG, NU, SLICE + TAIL, HD), bf),
            dma((3,)), dma((2 * HPG + 2,)),
            dma((1,)), dma((2, 2, HALF, HPG)),
            dma((1,)), dma((NZ, HPG)),
            dma((1,)), dma((HPG,)),
            dma((2,)), dma((2, HPG)),
        ],
        compiler_params=pltpu.CompilerParams(
            collective_id=0, has_side_effects=True, vmem_limit_bytes=54784 * 1024
        ),
    )(query, key_fresh, value_fresh, key_stale, value_stale)


def solution(mesh):
    spec = P(("patch", "uly"), None)
    return jax.shard_map(
        shards, mesh=mesh, in_specs=(spec,) * 5, out_specs=spec, check_vma=False,
    )
```

```python
import functools
import math

import jax
import jax.numpy as jnp
from jax import lax
from jax.experimental import pallas as pl
from jax.experimental.pallas import tpu as pltpu
from jax.sharding import PartitionSpec as P

HD = 128
HPG = 3
WIDTH = HPG * HD
NU = 8
NZ = 8
HALF = NZ // 2
SLICE = 48
SPAN = NU * SLICE
TAIL = 16
MESH = pl.DeviceIdType.MESH
C2 = HD ** (-0.5) * math.log2(math.e)


def slot_of(d, s):
    if s == 0:
        return 0
    if s == HALF:
        return HALF
    return s if d == 0 else HALF + s


def reach(t, d):
    return HALF if t == d else HALF - 1


TOPS = -1e30
NT = (((1,), (1,)), ((), ()))

PAIRS = (
    ((0, 1), (0, 5)), ((1, 1), (1, 5)), ((0, 2), (0, 6)), ((1, 2), (1, 6)), ((0, 3), (0, 7)),
    ((1, 3), (1, 7)), ((2, 1), (2, 5)), ((2, 2), (2, 6)), ((2, 3), (2, 7)),
)
CHUNK = 256


def pick(table, i):
    value = jnp.int32(table[0])
    for j in range(1, len(table)):
        value = jnp.where(i == j, jnp.int32(table[j]), value)
    return value


def kernel(q_in, kf_in, vf_in, ks_in, vs_in, out_ref,
           qbuf, kfb, vfb, kbuf, vbuf, acc, mx, ls, gives, takes,
           a2a_send, a2a_recv, ring_send, ring_recv, sib_send, sib_recv,
           qp_send, qp_recv, give_send, take_recv):
    patch = lax.axis_index("patch")
    u = lax.axis_index("uly")
    z = patch // 4
    yh = (patch // 2) % 2
    c = patch % 2
    up = ((z + 1) % NZ) * 4 + yh * 2 + c
    down = ((z + NZ - 1) % NZ) * 4 + yh * 2 + c
    sib = z * 4 + yh * 2 + (1 - c)
    par = z * 4 + (1 - yh) * 2 + c
    own0 = pl.multiple_of(c * SPAN, SPAN)
    sib0 = pl.multiple_of((1 - c) * SPAN, SPAN)
    crow = pl.ds(own0, SPAN)
    orow = pl.ds(sib0, SPAN)
    arow = pl.ds(0, SPAN)
    brow = pl.ds(SPAN, SPAN)

    barrier = pltpu.get_barrier_semaphore()
    for o in range(1, NU):
        pl.semaphore_signal(barrier, inc=1, device_id=(patch, (u + o) % NU), device_id_type=MESH)
    for p in (up, down, sib):
        pl.semaphore_signal(barrier, inc=1, device_id=(p, u), device_id_type=MESH)
    for o in range(NU):
        pl.semaphore_signal(barrier, inc=1, device_id=(par, (u + o) % NU), device_id_type=MESH)
    mx[...] = jnp.full_like(mx, TOPS)
    ls[...] = jnp.zeros_like(ls)
    acc[...] = jnp.zeros_like(acc)
    pl.semaphore_wait(barrier, 2 * NU - 1 + 3)

    def cols(h):
        return pl.ds(pl.multiple_of(h * HD, HD), HD)

    def bytes_of(ref, sem):
        return pltpu.make_async_copy(ref, ref, sem)

    own_rows = pl.ds(pl.multiple_of(u * SLICE, SLICE), SLICE)
    own_place = pl.ds(pl.multiple_of(c * SPAN + u * SLICE, SLICE), SLICE)

    def spread(src, dst, first, width, k, r):
        for o in range(1, NU):
            peer = (u + o) % NU
            pltpu.make_async_remote_copy(
                src_ref=src.at[:, pl.ds(pl.multiple_of(peer * WIDTH + first, HD), width)], dst_ref=dst,
                send_sem=a2a_send.at[k], recv_sem=a2a_recv.at[r], device_id=(patch, peer), device_id_type=MESH).start()
        pltpu.make_async_copy(
            src.at[:, pl.ds(pl.multiple_of(u * WIDTH + first, HD), width)], dst, a2a_recv.at[r]).start()

    def spread_stale(h):
        spread(ks_in, kbuf.at[0, own_place, cols(h)], h * HD, HD, 0, h)
        spread(vs_in, vbuf.at[0, own_place, cols(h)], h * HD, HD, 0, HPG + h)

    def spread_query(h):
        spread(q_in, qbuf.at[own_rows, cols(h)], h * HD, HD, 1, 2 * HPG + 1 + h)

    for h in range(HPG):
        spread_stale(h)
        spread_query(h)
    spread(kf_in, kfb.at[own_rows], 0, WIDTH, 2, 2 * HPG)
    spread(vf_in, vfb.at[own_rows], 0, WIDTH, 2, 2 * HPG)

    bufs = (kbuf, vbuf)

    def ring(t, d, s, h):
        return pltpu.make_async_remote_copy(
            src_ref=bufs[t].at[slot_of(d, s - 1), crow, cols(h)],
            dst_ref=bufs[t].at[slot_of(d, s), crow, cols(h)],
            send_sem=ring_send.at[0], recv_sem=ring_recv.at[t, d, s - 1, h],
            device_id=(up if d == 0 else down, u), device_id_type=MESH)

    def to_sib(t, slot, h):
        pltpu.make_async_remote_copy(
            src_ref=bufs[t].at[slot, crow, cols(h)], dst_ref=bufs[t].at[slot, crow, cols(h)],
            send_sem=sib_send.at[0], recv_sem=sib_recv.at[slot, h],
            device_id=(sib, u), device_id_type=MESH).start()

    def own_stale(h, t):
        bytes_of(bufs[t].at[0, crow, cols(h)], a2a_recv.at[t * HPG + h]).wait()

    FIRST, SECOND = ((0, 0), (1, 1)), ((1, 0), (0, 1))

    def inject(h):
        for t, d in FIRST + SECOND:
            ring(t, d, 1, h).start()

    def arrive(h, s, which=FIRST + SECOND):
        for t, d in which:
            if s > reach(t, d):
                continue
            ring(t, d, s, h).wait_recv()
            if s < reach(t, d):
                ring(t, d, s + 1, h).start()
            to_sib(t, slot_of(d, s), h)

    def q_par(h):
        return pltpu.make_async_remote_copy(
            src_ref=qbuf.at[arow, cols(h)], dst_ref=qbuf.at[brow, cols(h)],
            send_sem=qp_send.at[0], recv_sem=qp_recv.at[h], device_id=(par, u), device_id_type=MESH)

    def attend(h, r, k, v):
        n = k.shape[0]
        step = CHUNK if n % CHUNK == 0 else n
        for first in range(0, n, step):
            part_rows = pl.ds(first, step)
            s = lax.dot_general(qbuf[r, cols(h)], k[part_rows, :], NT, preferred_element_type=jnp.float32)
            m_old = mx[h, r, :]
            m_new = jnp.maximum(m_old, jnp.max(s, axis=1, keepdims=True))
            parts = [jnp.exp2((s[:, j * HD:(j + 1) * HD] - m_new) * C2) for j in range(step // HD)]
            tot = parts[0]
            for part in parts[1:]:
                tot = tot + part
            w = jnp.concatenate([part.astype(jnp.bfloat16) for part in parts], axis=1)
            pv = jnp.dot(w, v[part_rows, :], preferred_element_type=jnp.float32)
            alpha = jnp.exp2((m_old - m_new) * C2)
            mx[h, r, :] = m_new
            ls[h, r, :] = ls[h, r, :] * alpha + tot
            acc[h, r, :] = acc[h, r, :] * alpha + pv

    def block(h, slot, r):
        attend(h, r, kbuf.at[slot, :, cols(h)], vbuf.at[slot, :, cols(h)])

    tail_row = lax.broadcasted_iota(jnp.int32, (TAIL, HD), 0)
    diagonal = lax.broadcasted_iota(jnp.int32, (SLICE, HD), 0) == lax.broadcasted_iota(jnp.int32, (SLICE, HD), 1)

    def give(h, side):
        r = pl.ds(side * SPAN, SPAN)
        total = jnp.sum(ls[h, r, :], axis=1, keepdims=True)
        part = (acc[h, r, :] / total).astype(jnp.bfloat16)
        lse = mx[h, r, :] * C2 + jnp.log2(total)
        for p in range(NU):
            rows = slice(p * SLICE, (p + 1) * SLICE)
            line = jnp.sum(jnp.where(diagonal, lse[rows], 0.0), axis=0, keepdims=True)
            high = line.astype(jnp.bfloat16).astype(jnp.float32)
            middle = (line - high).astype(jnp.bfloat16).astype(jnp.float32)
            low = line - high - middle
            end = jnp.where(tail_row == 0, high, jnp.where(tail_row == 1, middle, jnp.where(tail_row == 2, low, 0.0)))
            gives[side, h, p, 0:SLICE, :] = part[rows]
            gives[side, h, p, SLICE:SLICE + TAIL, :] = end.astype(jnp.bfloat16)
        for o in range(NU):
            peer = (u + o) % NU
            if side == 0 and o == 0:
                pltpu.make_async_copy(gives.at[0, h, u], takes.at[0, h, u], take_recv.at[0, h]).start()
            else:
                pltpu.make_async_remote_copy(
                    src_ref=gives.at[side, h, peer], dst_ref=takes.at[side, h, u],
                    send_sem=give_send.at[side], recv_sem=take_recv.at[side, h],
                    device_id=(patch if side == 0 else par, peer), device_id_type=MESH).start()

    def merge(h):
        for side in range(2):
            bytes_of(takes.at[side, h], take_recv.at[side, h]).wait()
        for g in range(NU):
            sums, lses = [], []
            for side in range(2):
                sums.append(takes[side, h, g, 0:SLICE, :].astype(jnp.float32))
                end = takes[side, h, g, SLICE:SLICE + TAIL, :].astype(jnp.float32)
                line = jnp.sum(end, axis=0, keepdims=True)
                lses.append(jnp.sum(jnp.where(diagonal, line, 0.0), axis=1, keepdims=True))
            peak = jnp.maximum(lses[0], lses[1])
            wa = jnp.exp2(lses[0] - peak)
            wb = jnp.exp2(lses[1] - peak)
            both = (wa * sums[0] + wb * sums[1]) / (wa + wb)
            out_ref[:, (g * HPG + h) * HD:(g * HPG + h + 1) * HD] = both.astype(jnp.bfloat16)

    for t in range(2):
        own_stale(0, t)
        for d in range(2):
            ring(t, d, 1, 0).start()
        to_sib(t, 0, 0)
    bytes_of(qbuf.at[arow, cols(0)], a2a_recv.at[2 * HPG + 1]).wait()
    q_par(0).start()
    own_stale(1, 0)
    own_stale(1, 1)
    inject(1)
    for t in range(2):
        to_sib(t, 0, 1)
    arrive(0, 1)
    for h in range(1, HPG):
        bytes_of(qbuf.at[arow, cols(h)], a2a_recv.at[2 * HPG + 1 + h]).wait()
        q_par(h).start()
    for t in range(2):
        own_stale(2, t)
        to_sib(t, 0, 2)
    arrive(1, 1)
    q_par(0).wait_recv()

    def wait_sib(h, slot):
        bytes_of(kbuf.at[slot, :, cols(h)], sib_recv.at[slot, h]).wait()

    def own_chip(h):
        wait_sib(h, 0)
        attend(h, pl.ds(0, 2 * SPAN), kbuf.at[0, orow, cols(h)], vbuf.at[0, orow, cols(h)])
        attend(h, arow, kfb.at[:, cols(h)], vfb.at[:, cols(h)])
        attend(h, brow, kbuf.at[0, crow, cols(h)], vbuf.at[0, crow, cols(h)])

    def later():
        arrive(1, 2, SECOND)
        inject(2)
        bytes_of(kbuf.at[0], a2a_recv.at[2 * HPG]).wait()

    def last_block(h):
        arrive(h, HALF)
        wait_sib(h, HALF)
        block(h, HALF, pl.ds(0, 2 * SPAN))

    def between():
        last_block(0)
        give(0, 1)
        give(0, 0)
        last_block(1)
        give(1, 1)
        arrive(2, 2, FIRST)
        give(1, 0)
        arrive(2, 2, SECOND)

    before = {
        1: lambda: (arrive(0, 2), q_par(1).wait_recv()),
        2: lambda: arrive(1, 2, FIRST),
        3: later,
        4: lambda: (arrive(0, 3, SECOND), q_par(2).wait_recv()),
        5: lambda: arrive(1, 3, SECOND),
        6: lambda: arrive(2, 1, SECOND),
        7: between,
        8: lambda: (arrive(2, 3, FIRST), merge(0), arrive(2, 3, SECOND)),
    }

    def pair(i, carry):
        for j, event in before.items():
            pl.when(i == j)(lambda event=event: (event(), None)[1])
        pl.when((i >= 3) & (i < 3 + HPG))(lambda: own_chip(i - 3))
        for j, (h, s) in enumerate(((0, 3), (1, 3), (2, 1))):
            pl.when(i == 3 + j)(lambda h=h, s=s: arrive(h, s, FIRST))
        both = [(pick([p[g][0] for p in PAIRS], i), pick([p[g][1] for p in PAIRS], i)) for g in range(2)]
        for h, slot in both:
            wait_sib(h, slot)
        for h, slot in both:
            block(h, slot, pl.ds(0, 2 * SPAN))
        return carry

    lax.fori_loop(0, len(PAIRS), pair, 0)
    arrive(2, HALF)
    attend(2, pl.ds(0, 2 * SPAN), kbuf.at[HALF, crow, cols(2)], vbuf.at[HALF, crow, cols(2)])
    wait_sib(2, HALF)
    attend(2, brow, kbuf.at[HALF, orow, cols(2)], vbuf.at[HALF, orow, cols(2)])
    give(2, 1)
    attend(2, arow, kbuf.at[HALF, orow, cols(2)], vbuf.at[HALF, orow, cols(2)])
    give(2, 0)
    merge(1)
    merge(2)

    bytes_of(gives.at[0, :, pl.ds(0, NU - 1)], give_send.at[0]).wait()
    bytes_of(gives.at[1], give_send.at[1]).wait()
    bytes_of(qbuf.at[arow], qp_send.at[0]).wait()
    bytes_of(kbuf, sib_send.at[0]).wait()
    bytes_of(kbuf.at[pl.ds(0, NZ - 1)], ring_send.at[0]).wait()
    bytes_of(kbuf.at[0, pl.ds(0, 2 * (NU - 1) * SLICE)], a2a_send.at[0]).wait()
    bytes_of(qbuf.at[pl.ds(0, (NU - 1) * SLICE)], a2a_send.at[1]).wait()
    bytes_of(kbuf.at[0, pl.ds(0, 2 * (NU - 1) * SLICE)], a2a_send.at[2]).wait()


def shards(query, key_fresh, value_fresh, key_stale, value_stale):
    bf, f32 = jnp.bfloat16, jnp.float32
    dma = pltpu.SemaphoreType.DMA
    return pl.pallas_call(
        kernel,
        out_shape=jax.ShapeDtypeStruct(query.shape, bf),
        in_specs=[pl.BlockSpec(memory_space=pl.ANY)] * 5,
        out_specs=pl.BlockSpec(memory_space=pltpu.VMEM),
        scratch_shapes=[
            pltpu.VMEM((2 * SPAN, WIDTH), bf),
            pltpu.VMEM((SPAN, WIDTH), bf),
            pltpu.VMEM((SPAN, WIDTH), bf),
            pltpu.VMEM((NZ, 2 * SPAN, WIDTH), bf),
            pltpu.VMEM((NZ, 2 * SPAN, WIDTH), bf),
            pltpu.VMEM((HPG, 2 * SPAN, HD), f32),
            pltpu.VMEM((HPG, 2 * SPAN, HD), f32),
            pltpu.VMEM((HPG, 2 * SPAN, HD), f32),
            pltpu.VMEM((2, HPG, NU, SLICE + TAIL, HD), bf),
            pltpu.VMEM((2, HPG, NU, SLICE + TAIL, HD), bf),
            dma((3,)), dma((3 * HPG + 1,)),
            dma((1,)), dma((2, 2, HALF, HPG)),
            dma((1,)), dma((NZ, HPG)),
            dma((1,)), dma((HPG,)),
            dma((2,)), dma((2, HPG)),
        ],
        compiler_params=pltpu.CompilerParams(
            collective_id=0, has_side_effects=True, vmem_limit_bytes=54784 * 1024
        ),
    )(query, key_fresh, value_fresh, key_stale, value_stale)


def solution(mesh):
    spec = P(("patch", "uly"), None)
    return jax.shard_map(
        shards, mesh=mesh, in_specs=(spec,) * 5, out_specs=spec, check_vma=False,
    )
```

```python
import functools
import math

import jax
import jax.numpy as jnp
from jax import lax
from jax.experimental import pallas as pl
from jax.experimental.pallas import tpu as pltpu
from jax.sharding import PartitionSpec as P

HD = 128
HPG = 3
WIDTH = HPG * HD
NU = 8
NZ = 8
HALF = NZ // 2
SLICE = 48
SPAN = NU * SLICE
TAIL = 16
MESH = pl.DeviceIdType.MESH
C2 = HD ** (-0.5) * math.log2(math.e)


def slot_of(d, s):
    if s == 0:
        return 0
    if s == HALF:
        return HALF
    return s if d == 0 else HALF + s


def reach(t, d):
    return HALF if t == d else HALF - 1


TOPS = -1e30
NT = (((1,), (1,)), ((), ()))

PAIRS = (
    ((0, 1), (0, 5)), ((1, 1), (1, 5)), ((0, 2), (0, 6)), ((1, 2), (1, 6)), ((0, 3), (0, 7)),
    ((1, 3), (1, 7)), ((2, 1), (2, 5)), ((2, 2), (2, 6)), ((2, 3), (2, 7)),
)
CHUNK = 256


def pick(table, i):
    value = jnp.int32(table[0])
    for j in range(1, len(table)):
        value = jnp.where(i == j, jnp.int32(table[j]), value)
    return value


def kernel(q_in, kf_in, vf_in, ks_in, vs_in, out_ref,
           qbuf, kfb, vfb, kbuf, vbuf, acc, mx, ls, gives, takes,
           a2a_send, a2a_recv, ring_send, ring_recv, sib_send, sib_recv,
           qp_send, qp_recv, give_send, take_recv):
    patch = lax.axis_index("patch")
    u = lax.axis_index("uly")
    z = patch // 4
    yh = (patch // 2) % 2
    c = patch % 2
    up = ((z + 1) % NZ) * 4 + yh * 2 + c
    down = ((z + NZ - 1) % NZ) * 4 + yh * 2 + c
    sib = z * 4 + yh * 2 + (1 - c)
    par = z * 4 + (1 - yh) * 2 + c
    own0 = pl.multiple_of(c * SPAN, SPAN)
    sib0 = pl.multiple_of((1 - c) * SPAN, SPAN)
    crow = pl.ds(own0, SPAN)
    orow = pl.ds(sib0, SPAN)
    arow = pl.ds(0, SPAN)
    brow = pl.ds(SPAN, SPAN)

    barrier = pltpu.get_barrier_semaphore()
    for o in range(1, NU):
        pl.semaphore_signal(barrier, inc=1, device_id=(patch, (u + o) % NU), device_id_type=MESH)
    for p in (up, down, sib):
        pl.semaphore_signal(barrier, inc=1, device_id=(p, u), device_id_type=MESH)
    for o in range(NU):
        pl.semaphore_signal(barrier, inc=1, device_id=(par, (u + o) % NU), device_id_type=MESH)
    mx[...] = jnp.full_like(mx, TOPS)
    ls[...] = jnp.zeros_like(ls)
    acc[...] = jnp.zeros_like(acc)
    pl.semaphore_wait(barrier, 2 * NU - 1 + 3)

    def cols(h):
        return pl.ds(pl.multiple_of(h * HD, HD), HD)

    def bytes_of(ref, sem):
        return pltpu.make_async_copy(ref, ref, sem)

    own_rows = pl.ds(pl.multiple_of(u * SLICE, SLICE), SLICE)
    own_place = pl.ds(pl.multiple_of(c * SPAN + u * SLICE, SLICE), SLICE)

    def spread(src, dst, first, width, k, r):
        for o in range(1, NU):
            peer = (u + o) % NU
            pltpu.make_async_remote_copy(
                src_ref=src.at[:, pl.ds(pl.multiple_of(peer * WIDTH + first, HD), width)], dst_ref=dst,
                send_sem=a2a_send.at[k], recv_sem=a2a_recv.at[r], device_id=(patch, peer), device_id_type=MESH).start()
        pltpu.make_async_copy(
            src.at[:, pl.ds(pl.multiple_of(u * WIDTH + first, HD), width)], dst, a2a_recv.at[r]).start()

    def spread_stale(h):
        spread(ks_in, kbuf.at[0, own_place, cols(h)], h * HD, HD, 0, h)
        spread(vs_in, vbuf.at[0, own_place, cols(h)], h * HD, HD, 0, HPG + h)

    def spread_query(h):
        spread(q_in, qbuf.at[own_rows, cols(h)], h * HD, HD, 1, 2 * HPG + 1 + h)

    for h in range(HPG):
        spread_stale(h)
        spread_query(h)
    spread(kf_in, kfb.at[own_rows], 0, WIDTH, 2, 2 * HPG)
    spread(vf_in, vfb.at[own_rows], 0, WIDTH, 2, 2 * HPG)

    bufs = (kbuf, vbuf)

    def ring(t, d, s, h):
        return pltpu.make_async_remote_copy(
            src_ref=bufs[t].at[slot_of(d, s - 1), crow, cols(h)],
            dst_ref=bufs[t].at[slot_of(d, s), crow, cols(h)],
            send_sem=ring_send.at[0], recv_sem=ring_recv.at[t, d, s - 1, h],
            device_id=(up if d == 0 else down, u), device_id_type=MESH)

    def to_sib(t, slot, h):
        pltpu.make_async_remote_copy(
            src_ref=bufs[t].at[slot, crow, cols(h)], dst_ref=bufs[t].at[slot, crow, cols(h)],
            send_sem=sib_send.at[0], recv_sem=sib_recv.at[slot, h],
            device_id=(sib, u), device_id_type=MESH).start()

    def own_stale(h, t):
        bytes_of(bufs[t].at[0, crow, cols(h)], a2a_recv.at[t * HPG + h]).wait()

    FIRST, SECOND = ((0, 0), (1, 1)), ((1, 0), (0, 1))

    def inject(h):
        for t, d in FIRST + SECOND:
            ring(t, d, 1, h).start()

    def arrive(h, s, which=FIRST + SECOND):
        for t, d in which:
            if s > reach(t, d):
                continue
            ring(t, d, s, h).wait_recv()
            if s < reach(t, d):
                ring(t, d, s + 1, h).start()
            to_sib(t, slot_of(d, s), h)

    def q_par(h):
        return pltpu.make_async_remote_copy(
            src_ref=qbuf.at[arow, cols(h)], dst_ref=qbuf.at[brow, cols(h)],
            send_sem=qp_send.at[0], recv_sem=qp_recv.at[h], device_id=(par, u), device_id_type=MESH)

    def attend(h, r, k, v):
        n = k.shape[0]
        step = CHUNK if n % CHUNK == 0 else n
        for first in range(0, n, step):
            part_rows = pl.ds(first, step)
            s = lax.dot_general(qbuf[r, cols(h)], k[part_rows, :], NT, preferred_element_type=jnp.float32)
            m_old = mx[h, r, :]
            m_new = jnp.maximum(m_old, jnp.max(s, axis=1, keepdims=True))
            parts = [jnp.exp2((s[:, j * HD:(j + 1) * HD] - m_new) * C2) for j in range(step // HD)]
            tot = parts[0]
            for part in parts[1:]:
                tot = tot + part
            w = jnp.concatenate([part.astype(jnp.bfloat16) for part in parts], axis=1)
            pv = jnp.dot(w, v[part_rows, :], preferred_element_type=jnp.float32)
            alpha = jnp.exp2((m_old - m_new) * C2)
            mx[h, r, :] = m_new
            ls[h, r, :] = ls[h, r, :] * alpha + tot
            acc[h, r, :] = acc[h, r, :] * alpha + pv

    def block(h, slot, r):
        attend(h, r, kbuf.at[slot, :, cols(h)], vbuf.at[slot, :, cols(h)])

    tail_row = lax.broadcasted_iota(jnp.int32, (TAIL, HD), 0)
    diagonal = lax.broadcasted_iota(jnp.int32, (SLICE, HD), 0) == lax.broadcasted_iota(jnp.int32, (SLICE, HD), 1)

    def give(h, side):
        r = pl.ds(side * SPAN, SPAN)
        total = jnp.sum(ls[h, r, :], axis=1, keepdims=True)
        part = (acc[h, r, :] / total).astype(jnp.bfloat16)
        lse = mx[h, r, :] * C2 + jnp.log2(total)
        for p in range(NU):
            rows = slice(p * SLICE, (p + 1) * SLICE)
            line = jnp.sum(jnp.where(diagonal, lse[rows], 0.0), axis=0, keepdims=True)
            high = line.astype(jnp.bfloat16).astype(jnp.float32)
            middle = (line - high).astype(jnp.bfloat16).astype(jnp.float32)
            low = line - high - middle
            end = jnp.where(tail_row == 0, high, jnp.where(tail_row == 1, middle, jnp.where(tail_row == 2, low, 0.0)))
            gives[side, h, p, 0:SLICE, :] = part[rows]
            gives[side, h, p, SLICE:SLICE + TAIL, :] = end.astype(jnp.bfloat16)
        for o in range(NU):
            peer = (u + o) % NU
            if side == 0 and o == 0:
                pltpu.make_async_copy(gives.at[0, h, u], takes.at[0, h, u], take_recv.at[0, h]).start()
            else:
                pltpu.make_async_remote_copy(
                    src_ref=gives.at[side, h, peer], dst_ref=takes.at[side, h, u],
                    send_sem=give_send.at[side], recv_sem=take_recv.at[side, h],
                    device_id=(patch if side == 0 else par, peer), device_id_type=MESH).start()

    def merge(h):
        for side in range(2):
            bytes_of(takes.at[side, h], take_recv.at[side, h]).wait()
        for g in range(NU):
            sums, lses = [], []
            for side in range(2):
                sums.append(takes[side, h, g, 0:SLICE, :].astype(jnp.float32))
                end = takes[side, h, g, SLICE:SLICE + TAIL, :].astype(jnp.float32)
                line = jnp.sum(end, axis=0, keepdims=True)
                lses.append(jnp.sum(jnp.where(diagonal, line, 0.0), axis=1, keepdims=True))
            peak = jnp.maximum(lses[0], lses[1])
            wa = jnp.exp2(lses[0] - peak)
            wb = jnp.exp2(lses[1] - peak)
            both = (wa * sums[0] + wb * sums[1]) / (wa + wb)
            out_ref[:, (g * HPG + h) * HD:(g * HPG + h + 1) * HD] = both.astype(jnp.bfloat16)

    for t in range(2):
        own_stale(0, t)
        for d in range(2):
            ring(t, d, 1, 0).start()
        to_sib(t, 0, 0)
    bytes_of(qbuf.at[arow, cols(0)], a2a_recv.at[2 * HPG + 1]).wait()
    q_par(0).start()
    own_stale(1, 0)
    own_stale(1, 1)
    arrive(0, 1, FIRST)
    inject(1)
    for t in range(2):
        to_sib(t, 0, 1)
    arrive(0, 1, SECOND)
    for h in range(1, HPG):
        bytes_of(qbuf.at[arow, cols(h)], a2a_recv.at[2 * HPG + 1 + h]).wait()
        q_par(h).start()
    for t in range(2):
        own_stale(2, t)
        to_sib(t, 0, 2)
    arrive(1, 1)
    q_par(0).wait_recv()

    def wait_sib(h, slot):
        bytes_of(kbuf.at[slot, :, cols(h)], sib_recv.at[slot, h]).wait()

    def own_chip(h):
        wait_sib(h, 0)
        attend(h, pl.ds(0, 2 * SPAN), kbuf.at[0, orow, cols(h)], vbuf.at[0, orow, cols(h)])
        attend(h, arow, kfb.at[:, cols(h)], vfb.at[:, cols(h)])
        attend(h, brow, kbuf.at[0, crow, cols(h)], vbuf.at[0, crow, cols(h)])

    def later():
        arrive(1, 2, SECOND)
        inject(2)
        bytes_of(kbuf.at[0], a2a_recv.at[2 * HPG]).wait()

    def last_block(h):
        arrive(h, HALF)
        wait_sib(h, HALF)
        block(h, HALF, pl.ds(0, 2 * SPAN))

    def between():
        last_block(0)
        give(0, 1)
        give(0, 0)
        last_block(1)
        give(1, 1)
        arrive(2, 2, FIRST)
        give(1, 0)
        arrive(2, 2, SECOND)

    before = {
        1: lambda: (arrive(0, 2), q_par(1).wait_recv()),
        2: lambda: arrive(1, 2, FIRST),
        3: later,
        4: lambda: (arrive(0, 3, SECOND), q_par(2).wait_recv()),
        5: lambda: arrive(1, 3, SECOND),
        6: lambda: arrive(2, 1, SECOND),
        7: between,
        8: lambda: (arrive(2, 3, FIRST), merge(0), arrive(2, 3, SECOND)),
    }

    def pair(i, carry):
        for j, event in before.items():
            pl.when(i == j)(lambda event=event: (event(), None)[1])
        pl.when((i >= 3) & (i < 3 + HPG))(lambda: own_chip(i - 3))
        for j, (h, s) in enumerate(((0, 3), (1, 3), (2, 1))):
            pl.when(i == 3 + j)(lambda h=h, s=s: arrive(h, s, FIRST))
        both = [(pick([p[g][0] for p in PAIRS], i), pick([p[g][1] for p in PAIRS], i)) for g in range(2)]
        for h, slot in both:
            wait_sib(h, slot)
        for h, slot in both:
            block(h, slot, pl.ds(0, 2 * SPAN))
        return carry

    lax.fori_loop(0, len(PAIRS), pair, 0)
    arrive(2, HALF)
    attend(2, pl.ds(0, 2 * SPAN), kbuf.at[HALF, crow, cols(2)], vbuf.at[HALF, crow, cols(2)])
    wait_sib(2, HALF)
    attend(2, brow, kbuf.at[HALF, orow, cols(2)], vbuf.at[HALF, orow, cols(2)])
    give(2, 1)
    attend(2, arow, kbuf.at[HALF, orow, cols(2)], vbuf.at[HALF, orow, cols(2)])
    give(2, 0)
    merge(1)
    merge(2)

    bytes_of(gives.at[0, :, pl.ds(0, NU - 1)], give_send.at[0]).wait()
    bytes_of(gives.at[1], give_send.at[1]).wait()
    bytes_of(qbuf.at[arow], qp_send.at[0]).wait()
    bytes_of(kbuf, sib_send.at[0]).wait()
    bytes_of(kbuf.at[pl.ds(0, NZ - 1)], ring_send.at[0]).wait()
    bytes_of(kbuf.at[0, pl.ds(0, 2 * (NU - 1) * SLICE)], a2a_send.at[0]).wait()
    bytes_of(qbuf.at[pl.ds(0, (NU - 1) * SLICE)], a2a_send.at[1]).wait()
    bytes_of(kbuf.at[0, pl.ds(0, 2 * (NU - 1) * SLICE)], a2a_send.at[2]).wait()


def shards(query, key_fresh, value_fresh, key_stale, value_stale):
    bf, f32 = jnp.bfloat16, jnp.float32
    dma = pltpu.SemaphoreType.DMA
    return pl.pallas_call(
        kernel,
        out_shape=jax.ShapeDtypeStruct(query.shape, bf),
        in_specs=[pl.BlockSpec(memory_space=pl.ANY)] * 5,
        out_specs=pl.BlockSpec(memory_space=pltpu.VMEM),
        scratch_shapes=[
            pltpu.VMEM((2 * SPAN, WIDTH), bf),
            pltpu.VMEM((SPAN, WIDTH), bf),
            pltpu.VMEM((SPAN, WIDTH), bf),
            pltpu.VMEM((NZ, 2 * SPAN, WIDTH), bf),
            pltpu.VMEM((NZ, 2 * SPAN, WIDTH), bf),
            pltpu.VMEM((HPG, 2 * SPAN, HD), f32),
            pltpu.VMEM((HPG, 2 * SPAN, HD), f32),
            pltpu.VMEM((HPG, 2 * SPAN, HD), f32),
            pltpu.VMEM((2, HPG, NU, SLICE + TAIL, HD), bf),
            pltpu.VMEM((2, HPG, NU, SLICE + TAIL, HD), bf),
            dma((3,)), dma((3 * HPG + 1,)),
            dma((1,)), dma((2, 2, HALF, HPG)),
            dma((1,)), dma((NZ, HPG)),
            dma((1,)), dma((HPG,)),
            dma((2,)), dma((2, HPG)),
        ],
        compiler_params=pltpu.CompilerParams(
            collective_id=0, has_side_effects=True, vmem_limit_bytes=54784 * 1024
        ),
    )(query, key_fresh, value_fresh, key_stale, value_stale)


def solution(mesh):
    spec = P(("patch", "uly"), None)
    return jax.shard_map(
        shards, mesh=mesh, in_specs=(spec,) * 5, out_specs=spec, check_vma=False,
    )
```
